128 devices in a mesh: members: 4 (over y_hi, core), space: 32 (over y_lo, z, x).
Axes of the slice: x: 4, y: 4 (y_hi: 2, y_lo: 2; y = y_hi * 2 + y_lo), z: 4, core: 2. Of those that a mesh axis runs over, the one named last changes fastest.
Arguments:
- ensemble: float32 [3, 512, 256, 256], P(None, 'members', 'space'), may hold values from -6 to 6
- obs_cells: int32 [32, 4, 128], P('space', 'members'), may hold values from 0 to 1535
- obs_values: float32 [32, 4, 128], P('space', 'members'), may hold values from -6 to 6
- obs_var: float32 [32, 4, 128], P('space', 'members'), may hold values from 0.25 to 4
- obs_noise: float32 [512, 32, 4, 128], P(None, 'space', 'members'), may hold values from -6 to 6
- assign: int32 [512], replicated, may hold values from 0 to 511, each once
Outputs:
- analysis: float32 [3, 512, 256, 256], P(None, 'members', 'space')
The draws below stay inside these ranges and needn't reach their ends.
Inputs may be any that keep to these rules, and one draw needn't show every extreme that they name: assign holds every member once. obs_cells[r, c, k] = field * 8 * 64 + row * 64 + column within tile (r, c); repeats are possible.
All inputs are finite; a program needn't handle non-finite values.
Results may differ from the reference program's by a relative error of at most 0.0003.
Values sent between devices are 32-bit elements; how exact they have to be, the bound alone decides.
No kernel may reach another device: no remote copies, remote signals or barrier semaphores. Data moves between devices by JAX's collectives and lax.ppermute only.
A program may use at most 64 MiB of HBM per device.

```python
import math
import jax
import jax.numpy as jnp
from jax import lax

ROWS_DEV = 8
TILE_W = 64
STEPS = 4
OBS_TILE = 128
MEMBERS = 512
TILE_ROWS = 32
TILE_COLS = 4
NX = 256
NY = 256


def touch_ends(entries, own_key, low, top_value):
    extent = entries.shape
    spot = [jax.random.randint(jax.random.fold_in(own_key, axis), (), 0, extent[axis]) for axis in range(len(extent))]
    entries = entries.at[tuple(spot)].set(low)
    longest = extent.index(max(extent))
    spot[longest] = (spot[longest] + 1) % extent[longest]
    return entries.at[tuple(spot)].set(top_value)


def level_of(rng, shape, pieces, smallest, largest):
    gain = 1.0
    for axis_at, parts in pieces:
        heights = jax.random.uniform(jax.random.fold_in(jax.random.fold_in(rng, 6), axis_at), (parts,), jnp.float32, smallest / len(pieces), largest / len(pieces))
        gain = gain * jnp.repeat(jnp.exp(heights), shape[axis_at] // parts).reshape((-1,) + (1,) * (len(shape) - 1 - axis_at))
    return gain


def centred(own_key, shape, width, limit, pieces=(), held_as=jnp.bfloat16):
    factor_of = level_of(own_key, shape, pieces, -0.22, 0.18) if pieces else 1.0
    values = jax.random.normal(own_key, shape, jnp.float32) * width * factor_of
    return jnp.minimum(jnp.maximum(values, -limit), limit).astype(held_as)


def setup_inputs(seed: int = 0) -> dict:
    arg_keys = jax.random.split(jax.random.key(seed), 7)
    return {
        "ensemble": centred(arg_keys[0], (3, MEMBERS, NY, NX), 1.0, 6.0, ((1, 4), (2, 32)), jnp.float32),
        "obs_cells": touch_ends(jax.random.randint(arg_keys[1], (TILE_ROWS, TILE_COLS, OBS_TILE), 0, 3 * ROWS_DEV * TILE_W), jax.random.fold_in(arg_keys[1], 1), 0, (3 * ROWS_DEV * TILE_W) - 1).astype(jnp.int32),
        "obs_values": centred(arg_keys[2], (TILE_ROWS, TILE_COLS, OBS_TILE), 1.0, 6.0, ((0, 32), (1, 4)), jnp.float32),
        "obs_var": jnp.clip(jnp.exp(math.log(4.0) - 2.7725887 * jax.random.uniform(arg_keys[3], (TILE_ROWS, TILE_COLS, OBS_TILE), jnp.float32) ** level_of(arg_keys[3], (TILE_ROWS, TILE_COLS, OBS_TILE), ((0, 32), (1, 4)), -0.2, 0.2)), 0.25, 4.0),
        "obs_noise": centred(arg_keys[4], (MEMBERS, TILE_ROWS, TILE_COLS, OBS_TILE), 1.0, 6.0, ((1, 32), (2, 4)), jnp.float32),
        "assign": jax.random.permutation(arg_keys[5], MEMBERS).astype(jnp.int32),
    }


tstep = 0.1
gravity = 1.0
depth = 1.0
coriolis = 0.25
viscosity = 0.5

def centred_x(field):
    return 0.5 * (jnp.roll(field, -1, axis=2) - jnp.roll(field, 1, axis=2))

def height_update(state):
    eta, east, north = (state[0], state[1], state[2])
    column = depth + eta
    flux_x = centred_x(column * east)[:, 1:-1]
    carried = column * north
    flux_y = 0.5 * (carried[:, 2:] - carried[:, :-2])
    return eta[:, 1:-1] - tstep * (flux_x + flux_y)

def momentum_update(eta, east, north):

    def advance(field, extra):
        inner = field[:, 1:-1]
        grad_x = centred_x(field)[:, 1:-1]
        grad_y = 0.5 * (field[:, 2:] - field[:, :-2])
        spread = jnp.roll(field, -1, axis=2)[:, 1:-1] + jnp.roll(field, 1, axis=2)[:, 1:-1] + field[:, 2:] + field[:, :-2] - 4.0 * inner
        return inner + tstep * (-east[:, 1:-1] * grad_x - north[:, 1:-1] * grad_y + extra + viscosity * spread)
    slope_x = centred_x(eta)[:, 1:-1]
    slope_y = 0.5 * (eta[:, 2:] - eta[:, :-2])
    new_east = advance(east, coriolis * north[:, 1:-1] - gravity * slope_x)
    new_north = advance(north, -coriolis * east[:, 1:-1] - gravity * slope_y)
    return (new_east, new_north)

def pad_rows(state):
    return jnp.concatenate([state[:, :, -1:], state, state[:, :, :1]], axis=2)

def observe(tile, cells, values, variance, noise):
    tile_cells = tile.shape[2]
    field_of = cells // tile_cells
    cell_of = cells % tile_cells
    observed = tile[field_of, :, cell_of].T
    scale = 1.0 / jnp.sqrt(variance)
    mean_obs = lax.optimization_barrier(jnp.mean(observed, axis=0, keepdims=True))
    spread = (observed - mean_obs) * scale
    misfit = (values[None, :] - observed) * scale + noise
    return jnp.stack([spread, misfit])

def analyse_tile(tile, near):
    count = tile.shape[1]
    spread_all = jnp.transpose(near[:, :, 0], (2, 0, 1, 3)).reshape(count, -1)
    misfit_all = jnp.transpose(near[:, :, 1], (2, 0, 1, 3)).reshape(count, -1)
    gram = jnp.dot(spread_all, spread_all.T, precision=lax.Precision.HIGHEST) / (count - 1) + jnp.eye(count, dtype=jnp.float32)
    factor = jnp.linalg.cholesky(gram)
    reduced = jax.scipy.linalg.cho_solve((factor, True), spread_all)
    mixing = jnp.dot(misfit_all, reduced.T, precision=lax.Precision.HIGHEST) / (count - 1)
    anomaly = tile - lax.optimization_barrier(jnp.mean(tile, axis=1, keepdims=True))
    return tile + jnp.einsum('ij,fjc->fic', mixing, anomaly, precision=lax.Precision.HIGHEST)

def reference(ensemble, obs_cells, obs_values, obs_var, obs_noise, assign):
    state = ensemble
    for step in range(STEPS):
        eta_new = height_update(pad_rows(state))
        padded = pad_rows(jnp.stack([eta_new, state[1], state[2]]))
        east, north = momentum_update(padded[0], padded[1], padded[2])
        state = jnp.stack([eta_new, east, north])
    tiles = state.reshape(3, MEMBERS, TILE_ROWS, ROWS_DEV, TILE_COLS, TILE_W)
    tiles = tiles.transpose(2, 4, 0, 1, 3, 5).reshape(TILE_ROWS, TILE_COLS, 3, MEMBERS, ROWS_DEV * TILE_W)
    noise_all = jnp.take(obs_noise, assign, axis=0)
    noise_tiles = jnp.transpose(noise_all, (1, 2, 0, 3))
    packs = jax.vmap(jax.vmap(observe))(tiles, obs_cells, obs_values, obs_var, noise_tiles)

    def one_tile(index):
        row = index // TILE_COLS
        col = index % TILE_COLS
        offsets = jnp.arange(-1, 2, dtype=jnp.int32)
        rows = (row + offsets) % TILE_ROWS
        cols = (col + offsets) % TILE_COLS
        near = jnp.take(jnp.take(packs, rows, axis=0), cols, axis=1)
        return analyse_tile(tiles[row, col], near)
    done = lax.map(one_tile, jnp.arange(TILE_ROWS * TILE_COLS, dtype=jnp.int32))
    done = done.reshape(TILE_ROWS, TILE_COLS, 3, MEMBERS, ROWS_DEV, TILE_W)
    return done.transpose(2, 3, 0, 4, 1, 5).reshape(3, MEMBERS, NY, NX)
```

```python
import jax
import jax.numpy as jnp
from jax import lax
from jax.experimental import pallas as pl
from jax.experimental.pallas import tpu as pltpu
from jax.sharding import PartitionSpec as P

F32 = jnp.float32
BF16 = jnp.bfloat16
STEPS = 4
COUNT = 512
ROWS = 256
NEAR = 9
TSTEP = 0.1
DEPTH = 1.0
GRAVITY = 1.0
CORIOLIS = 0.25
VISCOSITY = 0.5
CHUNK = 8


def pair_shift(x):
    lane = lax.broadcasted_iota(jnp.int32, x.shape, 2)
    other = pltpu.roll(x, 4, 1)
    plus = pltpu.roll(jnp.where(lane == 0, other, x), 127, 2)
    minus = pltpu.roll(jnp.where(lane == 127, other, x), 1, 2)
    return plus, minus


def turned(parts):
    sub = lax.broadcasted_iota(jnp.int32, (8, 128), 0)
    for h in (4, 2, 1):
        upper = (sub & h) == 0
        result = list(parts)
        for i in range(8):
            if not i & h:
                a, b = parts[i], parts[i + h]
                result[i] = jnp.where(upper, a, pltpu.roll(b, h, 0))
                result[i + h] = jnp.where(upper, pltpu.roll(a, 8 - h, 0), b)
        parts = result
    return parts


def pack_kernel(ensemble, out):
    for d in range(4):
        for f in range(3):
            parts = [ensemble[f, 4 * d + k % 4, :, pl.ds(128 * (k // 4), 128)] for k in range(8)]
            for row, value in enumerate(turned(parts)):
                out[d, 8 * f + row] = value
        out[d, 24] = jnp.zeros((8, 128), F32)


def unpack_kernel(back, out):
    first = lax.broadcasted_iota(jnp.int32, (8, 128), 1) < 64

    def slots(i, carry):
        for f in range(3):
            for b in range(2):
                rows = []
                for row in range(0, 8, 2):
                    x = back[2 * b, pl.ds(8 * i, 8), pl.ds((8 * f + row) * 64, 128)]
                    y = back[2 * b + 1, pl.ds(8 * i, 8), pl.ds((8 * f + row) * 64, 128)]
                    rows.append(jnp.where(first, x, pltpu.roll(y, 64, 1)))
                    rows.append(jnp.where(first, pltpu.roll(x, 64, 1), y))
                for k, value in enumerate(turned(rows)):
                    out[f, 8 * i + k, :, pl.ds(128 * b, 128)] = value
        return carry

    lax.fori_loop(0, back.shape[1] // 8, slots, 0)


def forecast_kernel(got, obs_out, state_out, a_ref, b_ref, seen):
    def fill(t, carry):
        for f in range(3):
            a_ref[f, pl.ds(1 + 8 * t, 8)] = got[t, pl.ds(8 * f, 8)]
        return carry

    lax.fori_loop(0, 32, fill, 0)

    def wrap(ref, f):
        ref[f, 0] = ref[f, ROWS]
        ref[f, ROWS + 1] = ref[f, 1]

    for f in range(3):
        wrap(a_ref, f)

    def step(src, dst):
        def height(t, carry):
            at = t * CHUNK
            eta = src[0, pl.ds(at, CHUNK + 2)]
            column = DEPTH + eta
            plus, minus = pair_shift(column[1:-1] * src[1, pl.ds(at + 1, CHUNK)])
            carried = column * src[2, pl.ds(at, CHUNK + 2)]
            flux = (plus - minus) + (carried[2:] - carried[:-2])
            dst[0, pl.ds(at + 1, CHUNK)] = eta[1:-1] - (0.5 * TSTEP) * flux
            return carry

        lax.fori_loop(0, ROWS // CHUNK, height, 0, unroll=4)
        wrap(dst, 0)

        def momentum(t, carry):
            at = t * CHUNK
            eta = dst[0, pl.ds(at, CHUNK + 2)]
            east = src[1, pl.ds(at, CHUNK + 2)]
            north = src[2, pl.ds(at, CHUNK + 2)]
            eta_p, eta_m = pair_shift(eta[1:-1])
            e_in, n_in = east[1:-1], north[1:-1]

            def advance(field, inner, slope):
                plus, minus = pair_shift(inner)
                grad_x = plus - minus
                grad_y = field[2:] - field[:-2]
                around = plus + minus + field[2:] + field[:-2]
                force = around * (2.0 * VISCOSITY) - e_in * grad_x - n_in * grad_y - GRAVITY * slope
                return (1.0 - 4.0 * TSTEP * VISCOSITY) * inner + (0.5 * TSTEP) * force

            new_e = advance(east, e_in, eta_p - eta_m) + (TSTEP * CORIOLIS) * n_in
            new_n = advance(north, n_in, eta[2:] - eta[:-2]) - (TSTEP * CORIOLIS) * e_in
            dst[1, pl.ds(at + 1, CHUNK)] = new_e
            dst[2, pl.ds(at + 1, CHUNK)] = new_n
            return carry

        lax.fori_loop(0, ROWS // CHUNK, momentum, 0, unroll=4)
        wrap(dst, 1)
        wrap(dst, 2)

    def two_steps(t, carry):
        step(a_ref, b_ref)
        step(b_ref, a_ref)
        return carry

    lax.fori_loop(0, STEPS // 2, two_steps, 0)

    sub = lax.broadcasted_iota(jnp.int32, (8, 128), 0)
    lane = lax.broadcasted_iota(jnp.int32, (8, 128), 1)
    low = sub < 4
    first = lane < 64

    def tile_row(r, carry):
        rows = [a_ref[k // 8, 1 + 8 * r + k % 8] for k in range(24)]
        for p in range(2):
            cells = jnp.where(low, got[r, 24, pl.ds(p, 1)], got[r, 24, pl.ds(p + 2, 1)]).astype(jnp.int32)
            at = (cells & 63) + 64 * p
            which = cells >> 6
            value = jnp.zeros((8, 128), F32)
            for k in range(24):
                picked = jnp.take_along_axis(rows[k], at, axis=1, mode="promise_in_bounds")
                value = jnp.where(which == k, picked, value)
            seen[r, p, 0] = value
            seen[r, p, 1] = pltpu.roll(value, 4, 0)
        for j in range(6):
            v = rows[4 * j : 4 * j + 4]
            for p in range(2):
                halves = []
                for g in range(2):
                    x, y = v[2 * g], v[2 * g + 1]
                    if p == 0:
                        halves.append(jnp.where(first, x, pltpu.roll(y, 64, 1)))
                    else:
                        halves.append(jnp.where(first, pltpu.roll(x, 64, 1), y))
                x, y = halves
                state_out[p * 32 + r, :, pl.ds(128 * j, 128)] = jnp.where(low, x, pltpu.roll(y, 4, 0))
                state_out[(2 + p) * 32 + r, :, pl.ds(128 * j, 128)] = jnp.where(low, pltpu.roll(x, 4, 0), y)
        return carry

    lax.fori_loop(0, 32, tile_row, 0)

    def near_row(r, carry):
        for c in range(4):
            for j in range(5):
                half = []
                for g in range(2):
                    t = min(2 * j + g, NEAR - 1)
                    row = lax.rem(r + t // 3 + 31, 32)
                    other = (c + t % 3 + 3) % 4
                    half.append(seen[row, other % 2, int(other // 2 != g)])
                obs_out[c * 32 + r, :, pl.ds(128 * j, 128)] = jnp.where(low, half[0], half[1])
        return carry

    lax.fori_loop(0, 32, near_row, 0)


def by_member(msg, j, g):
    block = msg[:, :, pl.ds(128 * j, 128)].reshape(64, 2, 8, 128)
    x, y = block[:, 0], block[:, 1]
    low = lax.broadcasted_iota(jnp.int32, x.shape, 1) < 4
    if g == 0:
        out = jnp.where(low, x, pltpu.roll(y, 4, 1))
    else:
        out = jnp.where(low, pltpu.roll(x, 4, 1), y)
    return out.reshape(COUNT, 128)


def halves(x):
    high = x.astype(BF16)
    return high, (x - high.astype(F32)).astype(BF16)


def times(a, b):
    return lax.dot_general(a, b, (((1,), (0,)), ((), ())), preferred_element_type=F32)


def times_t(a, b):
    return lax.dot_general(a, b, (((1,), (1,)), ((), ())), preferred_element_type=F32)


def product(a, b, op):
    (ah, al), (bh, bl) = a, b
    return op(ah, bh) + (op(ah, bl) + op(al, bh))


def solve_kernel(obs, near_l, near_c, near_r, mix, sh, sl, mh, ml, gh, gl, xh, xl):
    for t in range(NEAR):
        seen = by_member(obs, t // 2, t % 2)
        extra = (near_l, near_c, near_r)[t % 3]
        row = t // 3
        noise = extra[row, 0:COUNT]
        values = extra[row, COUNT : COUNT + 1]
        scale = 1.0 / jnp.sqrt(extra[row, COUNT + 1 : COUNT + 2])
        mean = jnp.sum(seen, axis=0, keepdims=True) * (1.0 / COUNT)
        spread = (seen - mean) * scale
        misfit = (values - seen) * scale + noise
        at = pl.ds(128 * t, 128)
        sh[:, at], sl[:, at] = halves(spread)
        mh[:, at], ml[:, at] = halves(misfit)

    rows = lax.broadcasted_iota(jnp.int32, (COUNT, COUNT), 0)
    cols = lax.broadcasted_iota(jnp.int32, (COUNT, COUNT), 1)
    eye = (rows == cols).astype(F32)
    spread = (sh[...], sl[...])
    gram = product(spread, spread, times_t) * (1.0 / (COUNT - 1)) + eye
    gh[...], gl[...] = halves(gram)
    bound = jnp.max(jnp.sum(jnp.abs(gram), axis=1))
    alpha = 2.0 / (1.0 + bound)
    xh[...], xl[...] = halves(alpha * (2.0 * eye - alpha * gram))
    start = 4.0 * bound / ((1.0 + bound) * (1.0 + bound))

    def newton(scale):
        x = (xh[...], xl[...])
        t = product((gh[...], gl[...]), x, times)
        y = product(x, halves(t), times)
        full = x[0].astype(F32) + x[1].astype(F32)
        return scale * (2.0 * full - scale * y)

    def body(low):
        xh[...], xl[...] = halves(newton(2.0 / (1.0 + low)))
        return 4.0 * low / ((1.0 + low) * (1.0 + low))

    lax.while_loop(lambda low: low < 0.9999, body, start)
    inverse = newton(1.0)
    cross = product((mh[...], ml[...]), spread, times_t) * (1.0 / (COUNT - 1))
    mix[...] = product(halves(cross), halves(inverse), times)


def apply_kernel(state, mix, out):
    weights = halves(mix[...])
    for j in range(6):
        x = jnp.concatenate([by_member(state, j, 0), by_member(state, j, 1)], axis=1)
        mean = jnp.sum(x, axis=0, keepdims=True) * (1.0 / COUNT)
        out[:, pl.ds(256 * j, 256)] = x + product(weights, halves(x - mean), times)


def vmem(n):
    return [pl.BlockSpec(memory_space=pltpu.VMEM)] * n


def call(kernel, shapes, args, scratch=(), flops=0):
    return pl.pallas_call(
        kernel,
        out_shape=shapes,
        in_specs=vmem(len(args)),
        out_specs=vmem(len(shapes)) if isinstance(shapes, (list, tuple)) else vmem(1)[0],
        scratch_shapes=list(scratch),
        compiler_params=pltpu.CompilerParams(vmem_limit_bytes=52 * 1024 * 1024),
        cost_estimate=pl.CostEstimate(flops=flops, bytes_accessed=6_000_000, transcendentals=0),
    )(*args)


def around(x, axis):
    n = lax.axis_size(axis)
    ahead = [(i, (i + 1) % n) for i in range(n)]
    back = [((i + 1) % n, i) for i in range(n)]
    return lax.ppermute(x, axis, ahead), lax.ppermute(x, axis, back)


def local(ensemble, obs_cells, obs_values, obs_var, obs_noise, assign):
    everywhere = ("members", "space")
    me = lax.axis_index("members")
    own = obs_cells.reshape(1, 128).astype(F32)
    other = lax.ppermute(own, "members", [(0, 1), (1, 0), (2, 3), (3, 2)])
    pair = jnp.where(me % 2 == 0, jnp.concatenate([own, other]), jnp.concatenate([other, own]))
    other = lax.ppermute(pair, "members", [(0, 2), (2, 0), (1, 3), (3, 1)])
    cells = jnp.where(me < 2, jnp.concatenate([pair, other] * 2), jnp.concatenate([other, pair] * 2))
    send = pl.pallas_call(
        pack_kernel,
        out_shape=jax.ShapeDtypeStruct((32, 25, 8, 128), F32),
        grid=(8,),
        in_specs=[pl.BlockSpec((3, 16, 8, 256), lambda i: (0, i, 0, 0))],
        out_specs=pl.BlockSpec((4, 25, 8, 128), lambda i: (i, 0, 0, 0)),
    )(ensemble)
    send = send.at[:, 24].set(jnp.broadcast_to(cells, (32, 8, 128)))
    got = lax.all_to_all(send, "space", 0, 0, tiled=True)

    noise = jnp.take(obs_noise.reshape(COUNT, 128), assign, axis=0)
    extra = jnp.concatenate([noise, obs_values.reshape(1, 128), obs_var.reshape(1, 128), jnp.zeros((6, 128), F32)])
    above, below = around(extra, "space")
    near_c = jnp.stack([above, extra, below])
    got, near_c = lax.optimization_barrier((got, near_c))
    near_l, near_r = around(near_c, "members")

    obs_send, state_send = call(
        forecast_kernel,
        [jax.ShapeDtypeStruct((128, 8, 640), F32), jax.ShapeDtypeStruct((128, 8, 768), F32)],
        (got,),
        [pltpu.VMEM((3, ROWS + 2, 8, 128), F32)] * 2 + [pltpu.VMEM((32, 2, 2, 8, 128), F32)],
        flops=60_000_000,
    )
    obs_send, near_l, near_r = lax.optimization_barrier((obs_send, near_l, near_r))
    obs = lax.all_to_all(obs_send, everywhere, 0, 0, tiled=True)
    state_send, obs = lax.optimization_barrier((state_send, obs))
    state = lax.all_to_all(state_send, everywhere, 0, 0, tiled=True)
    mix = call(
        solve_kernel,
        jax.ShapeDtypeStruct((COUNT, COUNT), F32),
        (obs, near_l, near_c, near_r),
        [pltpu.VMEM((COUNT, 128 * NEAR), BF16)] * 4 + [pltpu.VMEM((COUNT, COUNT), BF16)] * 4,
        flops=20_000_000_000,
    )
    done = call(apply_kernel, jax.ShapeDtypeStruct((COUNT, 1536), F32), (state, mix), flops=3_000_000_000)
    back = lax.all_to_all(done.reshape(4, 128, 1536), "members", 0, 0, tiled=True)
    return pl.pallas_call(
        unpack_kernel,
        out_shape=jax.ShapeDtypeStruct((3, 128, 8, 256), F32),
        grid=(4,),
        in_specs=[pl.BlockSpec((4, 32, 1536), lambda i: (0, i, 0))],
        out_specs=pl.BlockSpec((3, 32, 8, 256), lambda i: (0, i, 0, 0)),
    )(back)


def solution(mesh):
    placed = (
        P(None, "members", "space", None),
        P("space", "members", None),
        P("space", "members", None),
        P("space", "members", None),
        P(None, "space", "members", None),
        P(),
    )
    return jax.shard_map(
        local,
        mesh=mesh,
        in_specs=placed,
        out_specs=P(None, "members", "space", None),
        check_vma=False,
    )
```

```python
import functools

import jax
import jax.numpy as jnp
from jax import lax
from jax.experimental import pallas as pl
from jax.experimental.pallas import tpu as pltpu
from jax.sharding import PartitionSpec as P

F32 = jnp.float32
BF16 = jnp.bfloat16
STEPS = 4
COUNT = 512
ROWS = 256
NEAR = 9
TSTEP = 0.1
DEPTH = 1.0
GRAVITY = 1.0
CORIOLIS = 0.25
VISCOSITY = 0.5
CHUNK = 8


def weigh(factor, x):
    return x if factor == 1.0 else factor * x


def pair_shift(x):
    lane = lax.broadcasted_iota(jnp.int32, x.shape, 2)
    other = pltpu.roll(x, 4, 1)
    plus = pltpu.roll(jnp.where(lane == 0, other, x), 127, 2)
    minus = pltpu.roll(jnp.where(lane == 127, other, x), 1, 2)
    return plus, minus


def turned(parts):
    sub = lax.broadcasted_iota(jnp.int32, (8, 128), 0)
    for h in (4, 2, 1):
        upper = (sub & h) == 0
        result = list(parts)
        for i in range(8):
            if not i & h:
                a, b = parts[i], parts[i + h]
                result[i] = jnp.where(upper, a, pltpu.roll(b, h, 0))
                result[i + h] = jnp.where(upper, pltpu.roll(a, 8 - h, 0), b)
        parts = result
    return parts


PACK = 8


def pack_kernel(ensemble, out, held, made, sem_in, sem_out):
    per = 32 // PACK
    incoming, outgoing = [], []
    for i in range(PACK):
        at = pl.ds(4 * per * i, 4 * per)
        incoming.append(pltpu.make_async_copy(ensemble.at[:, at], held.at[:, at], sem_in.at[i]))
        outgoing.append(pltpu.make_async_copy(made.at[pl.ds(per * i, per)], out.at[pl.ds(per * i, per)], sem_out.at[i]))
        incoming[i].start()
    for i in range(PACK):
        incoming[i].wait()
        for d in range(per * i, per * (i + 1)):
            for f in range(3):
                parts = [held[f, 4 * d + k % 4, :, pl.ds(128 * (k // 4), 128)] for k in range(8)]
                for row, value in enumerate(turned(parts)):
                    made[d, 8 * f + row] = value
            made[d, 24] = jnp.zeros((8, 128), F32)
        outgoing[i].start()
    for i in range(PACK):
        outgoing[i].wait()


def unpack_kernel(*refs):
    own, near, far, cross, out = refs[0], refs[1], refs[2], refs[3], refs[-1]
    first = lax.broadcasted_iota(jnp.int32, (8, 128), 1) < 64
    me = lax.axis_index("members")
    swapped = me % 2 == 1

    def slots(i, carry):
        at = pl.ds(8 * i, 8)
        for chip, (even, odd) in enumerate(((own, near), (far.at[0], cross))):
            rows = []
            for row in range(0, 8, 2):
                cut = pl.ds(row * 64, 128)
                u, v = even[at, cut], odd[at, cut]
                x, y = jnp.where(swapped, v, u), jnp.where(swapped, u, v)
                rows.append(jnp.where(first, x, pltpu.roll(y, 64, 1)))
                rows.append(jnp.where(first, pltpu.roll(x, 64, 1), y))
            place = pl.ds(pl.multiple_of(128 * ((me // 2) ^ chip), 128), 128)
            for k, value in enumerate(turned(rows)):
                out[0, 8 * i + k, :, place] = value
        return carry

    lax.fori_loop(0, 16, slots, 0, unroll=4)


def unpack(field, parts, out):
    held = [] if out is None else [out]
    return pl.pallas_call(
        unpack_kernel,
        out_shape=jax.ShapeDtypeStruct((3, 128, 8, 256), F32),
        grid=(1,),
        in_specs=[pl.BlockSpec(p.shape[-2:] if p.ndim == 2 else (1,) + p.shape[1:], lambda i, n=p.ndim: (0,) * n) for p in parts]
        + [pl.BlockSpec(memory_space=pl.ANY)] * len(held),
        out_specs=pl.BlockSpec((1, 128, 8, 256), lambda i: (field, 0, 0, 0)),
        input_output_aliases={4: 0} if held else {},
        cost_estimate=pl.CostEstimate(flops=1_000, bytes_accessed=1_000, transcendentals=0),
    )(*parts, *held)


def forecast_kernel(got, obs_out, state_out, a_ref, b_ref, seen):
    def fill(t, carry):
        for f in range(3):
            a_ref[f, pl.ds(1 + 8 * t, 8)] = got[t, pl.ds(8 * f, 8)]
        return carry

    lax.fori_loop(0, 32, fill, 0)

    def wrap(ref, f):
        ref[f, 0] = ref[f, ROWS]
        ref[f, ROWS + 1] = ref[f, 1]

    for f in range(3):
        wrap(a_ref, f)

    def step(src, dst):
        def height(t, carry):
            at = t * CHUNK
            eta = src[0, pl.ds(at, CHUNK + 2)]
            column = DEPTH + eta
            plus, minus = pair_shift(column[1:-1] * src[1, pl.ds(at + 1, CHUNK)])
            carried = column * src[2, pl.ds(at, CHUNK + 2)]
            flux = (plus - minus) + (carried[2:] - carried[:-2])
            dst[0, pl.ds(at + 1, CHUNK)] = eta[1:-1] - (0.5 * TSTEP) * flux
            return carry

        lax.fori_loop(0, ROWS // CHUNK, height, 0, unroll=8)
        wrap(dst, 0)

        def momentum(t, carry):
            at = t * CHUNK
            eta = dst[0, pl.ds(at, CHUNK + 2)]
            east = src[1, pl.ds(at, CHUNK + 2)]
            north = src[2, pl.ds(at, CHUNK + 2)]
            eta_p, eta_m = pair_shift(eta[1:-1])
            e_in, n_in = east[1:-1], north[1:-1]

            def advance(field, inner, slope):
                plus, minus = pair_shift(inner)
                grad_x = plus - minus
                grad_y = field[2:] - field[:-2]
                around = plus + minus + field[2:] + field[:-2]
                force = weigh(2.0 * VISCOSITY, around) - weigh(GRAVITY, slope) - (e_in * grad_x + n_in * grad_y)
                return (1.0 - 4.0 * TSTEP * VISCOSITY) * inner + (0.5 * TSTEP) * force

            new_e = advance(east, e_in, eta_p - eta_m) + (TSTEP * CORIOLIS) * n_in
            new_n = advance(north, n_in, eta[2:] - eta[:-2]) - (TSTEP * CORIOLIS) * e_in
            dst[1, pl.ds(at + 1, CHUNK)] = new_e
            dst[2, pl.ds(at + 1, CHUNK)] = new_n
            return carry

        lax.fori_loop(0, ROWS // CHUNK, momentum, 0, unroll=8)
        wrap(dst, 1)
        wrap(dst, 2)

    def two_steps(t, carry):
        step(a_ref, b_ref)
        step(b_ref, a_ref)
        return carry

    lax.fori_loop(0, STEPS // 2, two_steps, 0)

    sub = lax.broadcasted_iota(jnp.int32, (8, 128), 0)
    lane = lax.broadcasted_iota(jnp.int32, (8, 128), 1)
    low = sub < 4
    first = lane < 64

    def tile_row(r, carry):
        rows = [a_ref[k // 8, 1 + 8 * r + k % 8] for k in range(24)]
        for p in range(2):
            cells = jnp.where(low, got[r, 24, pl.ds(p, 1)], got[r, 24, pl.ds(p + 2, 1)]).astype(jnp.int32)
            at = (cells & 63) + 64 * p
            which = cells >> 6
            value = jnp.zeros((8, 128), F32)
            for k in range(24):
                picked = jnp.take_along_axis(rows[k], at, axis=1, mode="promise_in_bounds")
                value = jnp.where(which == k, picked, value)
            seen[r, p, 0] = value
            seen[r, p, 1] = pltpu.roll(value, 4, 0)
        for j in range(6):
            v = rows[4 * j : 4 * j + 4]
            for p in range(2):
                halves = []
                for g in range(2):
                    x, y = v[2 * g], v[2 * g + 1]
                    if p == 0:
                        halves.append(jnp.where(first, x, pltpu.roll(y, 64, 1)))
                    else:
                        halves.append(jnp.where(first, pltpu.roll(x, 64, 1), y))
                x, y = halves
                state_out[p * 32 + r, :, pl.ds(128 * j, 128)] = jnp.where(low, x, pltpu.roll(y, 4, 0))
                state_out[(2 + p) * 32 + r, :, pl.ds(128 * j, 128)] = jnp.where(low, pltpu.roll(x, 4, 0), y)
        return carry

    lax.fori_loop(0, 32, tile_row, 0, unroll=2)

    def near_row(r, carry):
        for c in range(4):
            outer = (c + 3) % 4 if c % 2 == 0 else (c + 1) % 4
            for j in range(3):
                half = []
                for g in range(2):
                    u = 2 * j + g
                    row = lax.rem(r + u % 3 + 31, 32)
                    tile = c if u < 3 else outer
                    half.append(seen[row, tile % 2, int(tile // 2 != g)])
                obs_out[c * 32 + r, :, pl.ds(128 * j, 128)] = jnp.where(low, half[0], half[1])
        return carry

    lax.fori_loop(0, 32, near_row, 0)


def by_member(msg, j, g):
    block = msg[:, :, pl.ds(128 * j, 128)].reshape(64, 2, 8, 128)
    x, y = block[:, 0], block[:, 1]
    low = lax.broadcasted_iota(jnp.int32, x.shape, 1) < 4
    if g == 0:
        out = jnp.where(low, x, pltpu.roll(y, 4, 1))
    else:
        out = jnp.where(low, pltpu.roll(x, 4, 1), y)
    return out.reshape(COUNT, 128)


def halves(x):
    high = x.astype(BF16)
    return high, (x - high.astype(F32)).astype(BF16)


def times(a, b):
    return lax.dot_general(a, b, (((1,), (0,)), ((), ())), preferred_element_type=F32)


def times_t(a, b):
    return lax.dot_general(a, b, (((1,), (1,)), ((), ())), preferred_element_type=F32)


def product(a, b, op):
    (ah, al), (bh, bl) = a, b
    return op(ah, bh) + (op(ah, bl) + op(al, bh))


def solve_kernel(obs, obs_core, near_c, near_out, near_core, mix_h, mix_l, sh, sl, mh, ml, gh, gl, xh, xl, near, sem):
    copies = [pltpu.make_async_copy(x, near.at[i], sem.at[i]) for i, x in enumerate((near_c, near_out, near_core))]
    for copy in copies:
        copy.start()
    for copy in copies:
        copy.wait()
    for t in range(NEAR):
        source, u = (obs, t) if t < 6 else (obs_core, t - 6)
        seen = by_member(source, u // 2, u % 2)
        place = t // 3, t % 3
        noise = near[place + (slice(0, COUNT),)]
        values = near[place + (slice(COUNT, COUNT + 1),)]
        scale = 1.0 / jnp.sqrt(near[place + (slice(COUNT + 1, COUNT + 2),)])
        mean = jnp.sum(seen, axis=0, keepdims=True) * (1.0 / COUNT)
        spread = (seen - mean) * scale
        misfit = (values - seen) * scale + noise
        at = pl.ds(128 * t, 128)
        sh[:, at], sl[:, at] = halves(spread)
        mh[:, at], ml[:, at] = halves(misfit)

    rows = lax.broadcasted_iota(jnp.int32, (COUNT, COUNT), 0)
    cols = lax.broadcasted_iota(jnp.int32, (COUNT, COUNT), 1)
    eye = (rows == cols).astype(F32)
    spread = (sh[...], sl[...])
    gram = product(spread, spread, times_t) * (1.0 / (COUNT - 1)) + eye
    gh[...], gl[...] = halves(gram)
    bound = jnp.max(jnp.sum(jnp.abs(gram), axis=1))
    alpha = 2.0 / (1.0 + bound)
    xh[...], xl[...] = halves(alpha * (2.0 * eye - alpha * gram))
    start = 4.0 * bound / ((1.0 + bound) * (1.0 + bound))

    def newton(scale):
        x = (xh[...], xl[...])
        t = product((gh[...], gl[...]), x, times)
        y = product(x, halves(t), times)
        full = x[0].astype(F32) + x[1].astype(F32)
        return scale * (2.0 * full - scale * y)

    def body(low):
        xh[...], xl[...] = halves(newton(2.0 / (1.0 + low)))
        return 4.0 * low / ((1.0 + low) * (1.0 + low))

    lax.while_loop(lambda low: low < 0.9999, body, start)
    inverse = newton(1.0)
    cross = product((mh[...], ml[...]), spread, times_t) * (1.0 / (COUNT - 1))
    rows_of = product(halves(cross), halves(inverse), times) + eye
    me = lax.axis_index("members")
    for k in range(4):
        block = rows_of[128 * k : 128 * (k + 1)]
        at = pl.ds(pl.multiple_of(128 * (me ^ k), 128), 128)
        mix_h[at], mix_l[at] = halves(block)


def apply_kernel(state, mix_h, mix_l, keep, near, far):
    weights = (mix_h[...], mix_l[...])
    for j in range(2):
        x = jnp.concatenate([by_member(state, j, 0), by_member(state, j, 1)], axis=1)
        mean = jnp.sum(x, axis=0, keepdims=True) * (1.0 / COUNT)
        done = mean + product(weights, halves(x - mean), times)
        cut = pl.ds(256 * j, 256)
        keep[:, cut] = done[0:128]
        near[:, cut] = done[128:256]
        far[0, :, cut] = done[256:384]
        far[1, :, cut] = done[384:512]


def apply(field, state, mix):
    block = jax.ShapeDtypeStruct((128, 512), F32)
    whole = pl.BlockSpec((COUNT, COUNT), lambda i: (0, 0))
    flat = pl.BlockSpec((128, 512), lambda i: (0, 0))
    return pl.pallas_call(
        apply_kernel,
        out_shape=[block, block, jax.ShapeDtypeStruct((2, 128, 512), F32)],
        grid=(1,),
        in_specs=[pl.BlockSpec((128, 8, 256), lambda i: (0, 0, field)), whole, whole],
        out_specs=[flat, flat, pl.BlockSpec((2, 128, 512), lambda i: (0, 0, 0))],
        compiler_params=pltpu.CompilerParams(vmem_limit_bytes=20 * 1024 * 1024),
        cost_estimate=pl.CostEstimate(flops=10_000_000_000, bytes_accessed=4_000_000, transcendentals=0),
    )(state, *mix)


def vmem(n):
    return [pl.BlockSpec(memory_space=pltpu.VMEM)] * n


def call(kernel, shapes, args, scratch=(), flops=0, mib=24, far=0):
    return pl.pallas_call(
        kernel,
        out_shape=shapes,
        in_specs=vmem(len(args) - far) + [pl.BlockSpec(memory_space=pl.ANY)] * far,
        out_specs=vmem(len(shapes)) if isinstance(shapes, (list, tuple)) else vmem(1)[0],
        scratch_shapes=list(scratch),
        compiler_params=pltpu.CompilerParams(vmem_limit_bytes=mib * 1024 * 1024),
        cost_estimate=pl.CostEstimate(flops=flops, bytes_accessed=6_000_000, transcendentals=0),
    )(*args)


def around(x, axis):
    n = lax.axis_size(axis)
    ahead = [(i, (i + 1) % n) for i in range(n)]
    back = [((i + 1) % n, i) for i in range(n)]
    return lax.ppermute(x, axis, ahead), lax.ppermute(x, axis, back)


def local(ensemble, obs_cells, obs_values, obs_var, obs_noise, assign):
    everywhere = ("members", "space")
    me = lax.axis_index("members")
    own = obs_cells.reshape(1, 128).astype(F32)
    other = lax.ppermute(own, "members", [(0, 1), (1, 0), (2, 3), (3, 2)])
    pair = jnp.where(me % 2 == 0, jnp.concatenate([own, other]), jnp.concatenate([other, own]))
    other = lax.ppermute(pair, "members", [(0, 2), (2, 0), (1, 3), (3, 1)])
    cells = jnp.where(me < 2, jnp.concatenate([pair, other] * 2), jnp.concatenate([other, pair] * 2))
    send = pl.pallas_call(
        pack_kernel,
        out_shape=jax.ShapeDtypeStruct((32, 25, 8, 128), F32),
        in_specs=[pl.BlockSpec(memory_space=pl.ANY)],
        out_specs=pl.BlockSpec(memory_space=pl.ANY),
        scratch_shapes=[
            pltpu.VMEM((3, 128, 8, 256), F32),
            pltpu.VMEM((32, 25, 8, 128), F32),
            pltpu.SemaphoreType.DMA((PACK,)),
            pltpu.SemaphoreType.DMA((PACK,)),
        ],
        compiler_params=pltpu.CompilerParams(vmem_limit_bytes=24 * 1024 * 1024),
    )(ensemble)
    send = send.at[:, 24].set(jnp.broadcast_to(cells, (32, 8, 128)))
    got = lax.all_to_all(send, "space", 0, 0, tiled=True)

    noise = jnp.take(obs_noise.reshape(COUNT, 128), assign, axis=0)
    extra = jnp.concatenate([noise, obs_values.reshape(1, 128), obs_var.reshape(1, 128), jnp.zeros((6, 128), F32)])
    above, below = around(extra, "space")
    near_c = jnp.stack([above, extra, below])
    got, near_c = lax.optimization_barrier((got, near_c))
    core = [(0, 1), (1, 0), (2, 3), (3, 2)]
    chip = [(0, 2), (2, 0), (1, 3), (3, 1)]
    near_out = lax.ppermute(near_c, "members", [(0, 3), (3, 0), (1, 2), (2, 1)])
    near_core = lax.ppermute(near_c, "members", core)

    obs_send, state_send = call(
        forecast_kernel,
        [jax.ShapeDtypeStruct((128, 8, 384), F32), jax.ShapeDtypeStruct((128, 8, 768), F32)],
        (got,),
        [pltpu.VMEM((3, ROWS + 2, 8, 128), F32)] * 2 + [pltpu.VMEM((32, 2, 2, 8, 128), F32)],
        flops=60_000_000,
    )
    obs_send, near_out, near_core = lax.optimization_barrier((obs_send, near_out, near_core))
    obs = lax.all_to_all(obs_send, everywhere, 0, 0, tiled=True)
    state_send, obs = lax.optimization_barrier((state_send, obs))
    state = lax.all_to_all(state_send, everywhere, 0, 0, tiled=True)
    obs_core = lax.ppermute(obs[:, :, 0:256], "members", core)
    mix = call(
        solve_kernel,
        [jax.ShapeDtypeStruct((COUNT, COUNT), BF16)] * 2,
        (obs, obs_core, near_c, near_out, near_core),
        [pltpu.VMEM((COUNT, 128 * NEAR), BF16)] * 4
        + [pltpu.VMEM((COUNT, COUNT), BF16)] * 4
        + [pltpu.VMEM((3, 3, 520, 128), F32), pltpu.SemaphoreType.DMA((3,))],
        flops=20_000_000_000,
        far=3,
    )
    sets = []
    for field in range(3):
        keep, near, far = apply(field, state, mix)
        sets.append((keep, lax.ppermute(near, "members", core), lax.ppermute(far, "members", chip)))
    out = None
    for field, (keep, near, far) in enumerate(sets):
        if out is not None:
            far, out = lax.optimization_barrier((far, out))
        out = unpack(field, (keep, near, far, lax.ppermute(far[1], "members", core)), out)
    return out


def solution(mesh):
    placed = (
        P(None, "members", "space", None),
        P("space", "members", None),
        P("space", "members", None),
        P("space", "members", None),
        P(None, "space", "members", None),
        P(),
    )
    return jax.shard_map(
        local,
        mesh=mesh,
        in_specs=placed,
        out_specs=P(None, "members", "space", None),
        check_vma=False,
    )
```

```python
import functools

import jax
import jax.numpy as jnp
from jax import lax
from jax.experimental import pallas as pl
from jax.experimental.pallas import tpu as pltpu
from jax.sharding import PartitionSpec as P

F32 = jnp.float32
BF16 = jnp.bfloat16
STEPS = 4
COUNT = 512
ROWS = 256
NEAR = 9
TSTEP = 0.1
DEPTH = 1.0
GRAVITY = 1.0
CORIOLIS = 0.25
VISCOSITY = 0.5
CHUNK = 8


def weigh(factor, x):
    return x if factor == 1.0 else factor * x


def pair_shift(x):
    lane = lax.broadcasted_iota(jnp.int32, x.shape, 2)
    other = pltpu.roll(x, 4, 1)
    plus = pltpu.roll(jnp.where(lane == 0, other, x), 127, 2)
    minus = pltpu.roll(jnp.where(lane == 127, other, x), 1, 2)
    return plus, minus


def turned(parts):
    sub = lax.broadcasted_iota(jnp.int32, (8, 128), 0)
    for h in (4, 2, 1):
        upper = (sub & h) == 0
        result = list(parts)
        for i in range(8):
            if not i & h:
                a, b = parts[i], parts[i + h]
                result[i] = jnp.where(upper, a, pltpu.roll(b, h, 0))
                result[i + h] = jnp.where(upper, pltpu.roll(a, 8 - h, 0), b)
        parts = result
    return parts


PACK = 8


def pack_kernel(ensemble, out, held, made, sem_in, sem_out):
    per = 32 // PACK
    incoming, outgoing = [], []
    for i in range(PACK):
        at = pl.ds(4 * per * i, 4 * per)
        incoming.append(pltpu.make_async_copy(ensemble.at[:, at], held.at[:, at], sem_in.at[i]))
        outgoing.append(pltpu.make_async_copy(made.at[pl.ds(per * i, per)], out.at[pl.ds(per * i, per)], sem_out.at[i]))
        incoming[i].start()
    for i in range(PACK):
        incoming[i].wait()
        for d in range(per * i, per * (i + 1)):
            for f in range(3):
                parts = [held[f, 4 * d + k % 4, :, pl.ds(128 * (k // 4), 128)] for k in range(8)]
                for row, value in enumerate(turned(parts)):
                    made[d, 8 * f + row] = value
            made[d, 24] = jnp.zeros((8, 128), F32)
        outgoing[i].start()
    for i in range(PACK):
        outgoing[i].wait()


def unpack_kernel(*refs):
    own, near, far, cross = (x if len(x.shape) == 2 else x.at[0] for x in refs[:4])
    out = refs[-1]
    first = lax.broadcasted_iota(jnp.int32, (8, 128), 1) < 64
    me = lax.axis_index("members")
    swapped = me % 2 == 1

    def slots(i, carry):
        at = pl.ds(8 * i, 8)
        for chip, (even, odd) in enumerate(((own, near), (far, cross))):
            rows = []
            for row in range(0, 8, 2):
                cut = pl.ds(row * 64, 128)
                u, v = even[at, cut], odd[at, cut]
                x, y = jnp.where(swapped, v, u), jnp.where(swapped, u, v)
                rows.append(jnp.where(first, x, pltpu.roll(y, 64, 1)))
                rows.append(jnp.where(first, pltpu.roll(x, 64, 1), y))
            place = pl.ds(pl.multiple_of(128 * ((me // 2) ^ chip), 128), 128)
            for k, value in enumerate(turned(rows)):
                out[0, 8 * i + k, :, place] = value
        return carry

    lax.fori_loop(0, 8, slots, 0, unroll=4)


def unpack(field, parts, out):
    held = [] if out is None else [out]
    return pl.pallas_call(
        unpack_kernel,
        out_shape=jax.ShapeDtypeStruct((3, 128, 8, 256), F32),
        grid=(2,),
        in_specs=[
            pl.BlockSpec((64, 512), lambda i: (i, 0))
            if k is None
            else pl.BlockSpec((1, 64, 512), lambda i, k=k: (k, i, 0))
            for _, k in parts
        ]
        + [pl.BlockSpec(memory_space=pl.ANY)] * len(held),
        out_specs=pl.BlockSpec((1, 64, 8, 256), lambda i: (field, i, 0, 0)),
        input_output_aliases={4: 0} if held else {},
        compiler_params=pltpu.CompilerParams(vmem_limit_bytes=12 * 1024 * 1024),
        cost_estimate=pl.CostEstimate(flops=1_000, bytes_accessed=1_000, transcendentals=0),
    )(*(p for p, _ in parts), *held)


def forecast_kernel(got, obs_out, state_out, a_ref, b_ref, seen):
    def fill(t, carry):
        for f in range(3):
            a_ref[f, pl.ds(1 + 8 * t, 8)] = got[t, pl.ds(8 * f, 8)]
        return carry

    lax.fori_loop(0, 32, fill, 0)

    def wrap(ref, f):
        ref[f, 0] = ref[f, ROWS]
        ref[f, ROWS + 1] = ref[f, 1]

    for f in range(3):
        wrap(a_ref, f)

    def step(src, dst):
        def height(t, carry):
            at = t * CHUNK
            eta = src[0, pl.ds(at, CHUNK + 2)]
            column = DEPTH + eta
            plus, minus = pair_shift(column[1:-1] * src[1, pl.ds(at + 1, CHUNK)])
            carried = column * src[2, pl.ds(at, CHUNK + 2)]
            flux = (plus - minus) + (carried[2:] - carried[:-2])
            dst[0, pl.ds(at + 1, CHUNK)] = eta[1:-1] - (0.5 * TSTEP) * flux
            return carry

        lax.fori_loop(0, ROWS // CHUNK, height, 0, unroll=16)
        wrap(dst, 0)

        def momentum(t, carry):
            at = t * CHUNK
            eta = dst[0, pl.ds(at, CHUNK + 2)]
            east = src[1, pl.ds(at, CHUNK + 2)]
            north = src[2, pl.ds(at, CHUNK + 2)]
            eta_p, eta_m = pair_shift(eta[1:-1])
            e_in, n_in = east[1:-1], north[1:-1]

            def advance(field, inner, slope):
                plus, minus = pair_shift(inner)
                grad_x = plus - minus
                grad_y = field[2:] - field[:-2]
                around = plus + minus + field[2:] + field[:-2]
                force = weigh(2.0 * VISCOSITY, around) - weigh(GRAVITY, slope) - (e_in * grad_x + n_in * grad_y)
                return (1.0 - 4.0 * TSTEP * VISCOSITY) * inner + (0.5 * TSTEP) * force

            new_e = advance(east, e_in, eta_p - eta_m) + (TSTEP * CORIOLIS) * n_in
            new_n = advance(north, n_in, eta[2:] - eta[:-2]) - (TSTEP * CORIOLIS) * e_in
            dst[1, pl.ds(at + 1, CHUNK)] = new_e
            dst[2, pl.ds(at + 1, CHUNK)] = new_n
            return carry

        lax.fori_loop(0, ROWS // CHUNK, momentum, 0, unroll=16)
        wrap(dst, 1)
        wrap(dst, 2)

    def two_steps(t, carry):
        step(a_ref, b_ref)
        step(b_ref, a_ref)
        return carry

    lax.fori_loop(0, STEPS // 2, two_steps, 0)

    sub = lax.broadcasted_iota(jnp.int32, (8, 128), 0)
    lane = lax.broadcasted_iota(jnp.int32, (8, 128), 1)
    low = sub < 4
    first = lane < 64

    def tile_row(r, carry):
        rows = [a_ref[k // 8, 1 + 8 * r + k % 8] for k in range(24)]
        for p in range(2):
            cells = jnp.where(low, got[r, 24, pl.ds(p, 1)], got[r, 24, pl.ds(p + 2, 1)]).astype(jnp.int32)
            at = (cells & 63) + 64 * p
            which = cells >> 6
            value = jnp.zeros((8, 128), F32)
            for k in range(24):
                picked = jnp.take_along_axis(rows[k], at, axis=1, mode="promise_in_bounds")
                value = jnp.where(which == k, picked, value)
            seen[r, p, 0] = value
            seen[r, p, 1] = pltpu.roll(value, 4, 0)
        for j in range(6):
            v = rows[4 * j : 4 * j + 4]
            for p in range(2):
                halves = []
                for g in range(2):
                    x, y = v[2 * g], v[2 * g + 1]
                    if p == 0:
                        halves.append(jnp.where(first, x, pltpu.roll(y, 64, 1)))
                    else:
                        halves.append(jnp.where(first, pltpu.roll(x, 64, 1), y))
                x, y = halves
                state_out[p * 32 + r, :, pl.ds(128 * j, 128)] = jnp.where(low, x, pltpu.roll(y, 4, 0))
                state_out[(2 + p) * 32 + r, :, pl.ds(128 * j, 128)] = jnp.where(low, pltpu.roll(x, 4, 0), y)
        return carry

    lax.fori_loop(0, 32, tile_row, 0, unroll=4)

    def near_row(r, carry):
        for c in range(4):
            outer = (c + 3) % 4 if c % 2 == 0 else (c + 1) % 4
            for j in range(3):
                half = []
                for g in range(2):
                    u = 2 * j + g
                    row = lax.rem(r + u % 3 + 31, 32)
                    tile = c if u < 3 else outer
                    half.append(seen[row, tile % 2, int(tile // 2 != g)])
                obs_out[c * 32 + r, :, pl.ds(128 * j, 128)] = jnp.where(low, half[0], half[1])
        return carry

    lax.fori_loop(0, 32, near_row, 0)


def by_member(msg, j, g):
    block = msg[:, :, pl.ds(128 * j, 128)].reshape(64, 2, 8, 128)
    x, y = block[:, 0], block[:, 1]
    low = lax.broadcasted_iota(jnp.int32, x.shape, 1) < 4
    if g == 0:
        out = jnp.where(low, x, pltpu.roll(y, 4, 1))
    else:
        out = jnp.where(low, pltpu.roll(x, 4, 1), y)
    return out.reshape(COUNT, 128)


def halves(x):
    high = x.astype(BF16)
    return high, (x - high.astype(F32)).astype(BF16)


def times(a, b):
    return lax.dot_general(a, b, (((1,), (0,)), ((), ())), preferred_element_type=F32)


def times_t(a, b):
    return lax.dot_general(a, b, (((1,), (1,)), ((), ())), preferred_element_type=F32)


def full(a, b):
    return jnp.dot(a, b, precision=lax.Precision.HIGHEST, preferred_element_type=F32)


def full_t(a, b):
    dims = (((1,), (1,)), ((), ()))
    return lax.dot_general(a, b, dims, precision=lax.Precision.HIGHEST, preferred_element_type=F32)


def product(a, b, op):
    (ah, al), (bh, bl) = a, b
    return op(ah, bh) + (op(ah, bl) + op(al, bh))


def solve_kernel(obs, obs_core, c_mid, c_side, o_mid, o_side, p_mid, p_side, mix, *scratch):
    spread, misfit, gh, gl, xh, xl, near, sem = scratch
    copies = []
    for i, (mid, side) in enumerate(((c_mid, c_side), (o_mid, o_side), (p_mid, p_side))):
        for row, source in enumerate((side.at[0], mid, side.at[1])):
            copies.append(pltpu.make_async_copy(source, near.at[i, row], sem.at[3 * i + row]))
    for copy in copies:
        copy.start()
    for copy in copies:
        copy.wait()
    for t in range(NEAR):
        source, u = (obs, t) if t < 6 else (obs_core, t - 6)
        seen = by_member(source, u // 2, u % 2)
        place = t // 3, t % 3
        noise = near[place + (slice(0, COUNT),)]
        values = near[place + (slice(COUNT, COUNT + 1),)]
        scale = 1.0 / jnp.sqrt(near[place + (slice(COUNT + 1, COUNT + 2),)])
        mean = jnp.sum(seen, axis=0, keepdims=True) * (1.0 / COUNT)
        at = pl.ds(128 * t, 128)
        spread[:, at] = (seen - mean) * scale
        misfit[:, at] = (values - seen) * scale + noise

    rows = lax.broadcasted_iota(jnp.int32, (COUNT, COUNT), 0)
    cols = lax.broadcasted_iota(jnp.int32, (COUNT, COUNT), 1)
    eye = (rows == cols).astype(F32)
    gram = full_t(spread[...], spread[...]) * (1.0 / (COUNT - 1)) + eye
    gh[...], gl[...] = halves(gram)
    bound = jnp.max(jnp.sum(jnp.abs(gram), axis=1))
    alpha = 2.0 / (1.0 + bound)
    xh[...], xl[...] = halves(alpha * (2.0 * eye - alpha * gram))
    start = 4.0 * bound / ((1.0 + bound) * (1.0 + bound))

    def newton(scale):
        x = (xh[...], xl[...])
        t = product((gh[...], gl[...]), x, times)
        y = product(x, halves(t), times)
        full = x[0].astype(F32) + x[1].astype(F32)
        return scale * (2.0 * full - scale * y)

    def body(low):
        xh[...], xl[...] = halves(newton(2.0 / (1.0 + low)))
        return 4.0 * low / ((1.0 + low) * (1.0 + low))

    lax.while_loop(lambda low: low < 0.9999, body, start)
    inverse = newton(1.0)
    for _ in range(2):
        rest = eye - full(gram, inverse)
        inverse = inverse + product(halves(inverse), halves(rest), times)
    cross = full_t(misfit[...], spread[...]) * (1.0 / (COUNT - 1))
    rows_of = full(cross, inverse) + eye
    me = lax.axis_index("members")
    for k in range(4):
        block = rows_of[128 * k : 128 * (k + 1)]
        at = pl.ds(pl.multiple_of(128 * (me ^ k), 128), 128)
        mix[0, at], mix[1, at] = halves(block)


def apply_kernel(core_first, state, mix, keep, one, two):
    weights = (mix[0], mix[1])
    x = jnp.concatenate([by_member(state, 0, 0), by_member(state, 0, 1)], axis=1)
    mean = jnp.sum(x, axis=0, keepdims=True) * (1.0 / COUNT)
    done = mean + product(weights, halves(x - mean), times)
    lone, first = (256, 128) if core_first else (128, 256)
    keep[...] = done[0:128]
    one[...] = done[lone : lone + 128]
    two[0] = done[first : first + 128]
    two[1] = done[384:512]


def apply(field, state, mix, core_first=False):
    block = jax.ShapeDtypeStruct((128, 512), F32)
    whole = pl.BlockSpec((2, COUNT, COUNT), lambda i: (0, 0, 0))
    flat = pl.BlockSpec((128, 256), lambda i: (0, i))
    return pl.pallas_call(
        functools.partial(apply_kernel, core_first),
        out_shape=[block, block, jax.ShapeDtypeStruct((2, 128, 512), F32)],
        grid=(2,),
        in_specs=[pl.BlockSpec((128, 8, 128), lambda i: (0, 0, 2 * field + i)), whole],
        out_specs=[flat, flat, pl.BlockSpec((2, 128, 256), lambda i: (0, 0, i))],
        compiler_params=pltpu.CompilerParams(vmem_limit_bytes=60 * 1024 * 1024),
        cost_estimate=pl.CostEstimate(flops=10_000_000_000, bytes_accessed=4_000_000, transcendentals=0),
    )(state, mix)


def vmem(n):
    return [pl.BlockSpec(memory_space=pltpu.VMEM)] * n


def call(kernel, shapes, args, scratch=(), flops=0, mib=24, far=0):
    return pl.pallas_call(
        kernel,
        out_shape=shapes,
        in_specs=vmem(len(args) - far) + [pl.BlockSpec(memory_space=pl.ANY)] * far,
        out_specs=vmem(len(shapes)) if isinstance(shapes, (list, tuple)) else vmem(1)[0],
        scratch_shapes=list(scratch),
        compiler_params=pltpu.CompilerParams(vmem_limit_bytes=mib * 1024 * 1024),
        cost_estimate=pl.CostEstimate(flops=flops, bytes_accessed=6_000_000, transcendentals=0),
    )(*args)


def around(x, axis):
    n = lax.axis_size(axis)
    ahead = [(i, (i + 1) % n) for i in range(n)]
    back = [((i + 1) % n, i) for i in range(n)]
    return lax.ppermute(x, axis, ahead), lax.ppermute(x, axis, back)


def local(ensemble, obs_cells, obs_values, obs_var, obs_noise, assign):
    everywhere = ("members", "space")
    me = lax.axis_index("members")
    own = obs_cells.reshape(1, 128).astype(F32)
    other = lax.ppermute(own, "members", [(0, 1), (1, 0), (2, 3), (3, 2)])
    pair = jnp.where(me % 2 == 0, jnp.concatenate([own, other]), jnp.concatenate([other, own]))
    other = lax.ppermute(pair, "members", [(0, 2), (2, 0), (1, 3), (3, 1)])
    cells = jnp.where(me < 2, jnp.concatenate([pair, other] * 2), jnp.concatenate([other, pair] * 2))
    send = pl.pallas_call(
        pack_kernel,
        out_shape=jax.ShapeDtypeStruct((32, 25, 8, 128), F32),
        in_specs=[pl.BlockSpec(memory_space=pl.ANY)],
        out_specs=pl.BlockSpec(memory_space=pl.ANY),
        scratch_shapes=[
            pltpu.VMEM((3, 128, 8, 256), F32),
            pltpu.VMEM((32, 25, 8, 128), F32),
            pltpu.SemaphoreType.DMA((PACK,)),
            pltpu.SemaphoreType.DMA((PACK,)),
        ],
        compiler_params=pltpu.CompilerParams(vmem_limit_bytes=60 * 1024 * 1024),
    )(ensemble)
    send = send.at[:, 24].set(jnp.broadcast_to(cells, (32, 8, 128)))
    got = lax.all_to_all(send, "space", 0, 0, tiled=True)

    noise = jnp.take(obs_noise.reshape(COUNT, 128), assign, axis=0)
    extra = jnp.concatenate([noise, obs_values.reshape(1, 128), obs_var.reshape(1, 128), jnp.zeros((6, 128), F32)])
    core = [(0, 1), (1, 0), (2, 3), (3, 2)]
    chip = [(0, 2), (2, 0), (1, 3), (3, 1)]
    outer = [(0, 3), (3, 0), (1, 2), (2, 1)]
    sides = jnp.stack(around(extra, "space"))
    extra_out = lax.ppermute(extra, "members", outer)
    extra_core = lax.ppermute(extra, "members", core)
    got, sides, extra_out, extra_core = lax.optimization_barrier((got, sides, extra_out, extra_core))
    sides_out = lax.ppermute(sides, "members", outer)
    sides_core = lax.ppermute(sides, "members", core)

    obs_send, state_send = call(
        forecast_kernel,
        [jax.ShapeDtypeStruct((128, 8, 384), F32), jax.ShapeDtypeStruct((128, 8, 768), F32)],
        (got,),
        [pltpu.VMEM((3, ROWS + 2, 8, 128), F32)] * 2 + [pltpu.VMEM((32, 2, 2, 8, 128), F32)],
        flops=60_000_000,
    )
    obs_send, sides_out, sides_core = lax.optimization_barrier((obs_send, sides_out, sides_core))
    obs = lax.all_to_all(obs_send, everywhere, 0, 0, tiled=True)
    state_send, obs = lax.optimization_barrier((state_send, obs))
    state = lax.all_to_all(state_send, everywhere, 0, 0, tiled=True)
    obs_core = lax.ppermute(obs[:, :, 0:256], "members", core)
    mix = call(
        solve_kernel,
        jax.ShapeDtypeStruct((2, COUNT, COUNT), BF16),
        (obs, obs_core, extra, sides, extra_out, sides_out, extra_core, sides_core),
        [pltpu.VMEM((COUNT, 128 * NEAR), F32)] * 2
        + [pltpu.VMEM((COUNT, COUNT), BF16)] * 4
        + [pltpu.VMEM((3, 3, 520, 128), F32), pltpu.SemaphoreType.DMA((9,))],
        flops=20_000_000_000,
        far=6,
        mib=32,
    )
    sets = []
    for field in range(2):
        keep, near, far = apply(field, state, mix)
        sets.append((keep, near, lax.ppermute(far, "members", chip)))
    keep, far, pair = apply(2, state, mix, core_first=True)
    pair = lax.ppermute(pair, "members", core)
    far = jnp.stack([far, pair[1]])
    last = lax.ppermute(far, "members", chip)
    far_0, _ = lax.optimization_barrier((sets[0][2], far))
    near_0, near_1, far_0 = lax.optimization_barrier((sets[0][1], sets[1][1], far_0))
    near_0 = lax.ppermute(near_0, "members", core)
    near_1 = lax.ppermute(near_1, "members", core)
    cross = lax.ppermute(far_0[1], "members", core)
    out = unpack(0, ((sets[0][0], None), (near_0, None), (far_0, 0), (cross, None)), None)
    far_1, out = lax.optimization_barrier((sets[1][2], out))
    cross = lax.ppermute(far_1[1], "members", core)
    out = unpack(1, ((sets[1][0], None), (near_1, None), (far_1, 0), (cross, None)), out)
    last, out = lax.optimization_barrier((last, out))
    return unpack(2, ((keep, None), (pair, 0), (last, 0), (last, 1)), out)


def solution(mesh):
    placed = (
        P(None, "members", "space", None),
        P("space", "members", None),
        P("space", "members", None),
        P("space", "members", None),
        P(None, "space", "members", None),
        P(),
    )
    return jax.shard_map(
        local,
        mesh=mesh,
        in_specs=placed,
        out_specs=P(None, "members", "space", None),
        check_vma=False,
    )
```

```python
import functools

import jax
import jax.numpy as jnp
from jax import lax
from jax.experimental import pallas as pl
from jax.experimental.pallas import tpu as pltpu
from jax.sharding import PartitionSpec as P

F32 = jnp.float32
BF16 = jnp.bfloat16
STEPS = 4
COUNT = 512
ROWS = 256
NEAR = 9
TSTEP = 0.1
DEPTH = 1.0
GRAVITY = 1.0
CORIOLIS = 0.25
VISCOSITY = 0.5
CHUNK = 8


def weigh(factor, x):
    return x if factor == 1.0 else factor * x


def pair_shift(x):
    lane = lax.broadcasted_iota(jnp.int32, x.shape, 2)
    other = pltpu.roll(x, 4, 1)
    plus = pltpu.roll(jnp.where(lane == 0, other, x), 127, 2)
    minus = pltpu.roll(jnp.where(lane == 127, other, x), 1, 2)
    return plus, minus


def turned(parts):
    sub = lax.broadcasted_iota(jnp.int32, (8, 128), 0)
    for h in (4, 2, 1):
        upper = (sub & h) == 0
        result = list(parts)
        for i in range(8):
            if not i & h:
                a, b = parts[i], parts[i + h]
                result[i] = jnp.where(upper, a, pltpu.roll(b, h, 0))
                result[i + h] = jnp.where(upper, pltpu.roll(a, 8 - h, 0), b)
        parts = result
    return parts


PACK = 8


def pack_kernel(ensemble, out, held, made, sem_in, sem_out):
    per = 32 // PACK
    incoming, outgoing = [], []
    for i in range(PACK):
        at = pl.ds(4 * per * i, 4 * per)
        incoming.append(pltpu.make_async_copy(ensemble.at[:, at], held.at[:, at], sem_in.at[i]))
        outgoing.append(pltpu.make_async_copy(made.at[pl.ds(per * i, per)], out.at[pl.ds(per * i, per)], sem_out.at[i]))
        incoming[i].start()
    for i in range(PACK):
        incoming[i].wait()
        for d in range(per * i, per * (i + 1)):
            for f in range(3):
                parts = [held[f, 4 * d + k % 4, :, pl.ds(128 * (k // 4), 128)] for k in range(8)]
                for row, value in enumerate(turned(parts)):
                    made[d, 8 * f + row] = value
            made[d, 24] = jnp.zeros((8, 128), F32)
        outgoing[i].start()
    for i in range(PACK):
        outgoing[i].wait()


def unpack_kernel(*refs):
    own, near, far, cross = (x if len(x.shape) == 2 else x.at[0] for x in refs[:4])
    out = refs[-1]
    first = lax.broadcasted_iota(jnp.int32, (8, 128), 1) < 64
    me = lax.axis_index("members")
    swapped = me % 2 == 1

    def slots(i, carry):
        at = pl.ds(8 * i, 8)
        for chip, (even, odd) in enumerate(((own, near), (far, cross))):
            rows = []
            for row in range(0, 8, 2):
                cut = pl.ds(row * 64, 128)
                u, v = even[at, cut], odd[at, cut]
                x, y = jnp.where(swapped, v, u), jnp.where(swapped, u, v)
                rows.append(jnp.where(first, x, pltpu.roll(y, 64, 1)))
                rows.append(jnp.where(first, pltpu.roll(x, 64, 1), y))
            place = pl.ds(pl.multiple_of(128 * ((me // 2) ^ chip), 128), 128)
            for k, value in enumerate(turned(rows)):
                out[0, 8 * i + k, :, place] = value
        return carry

    lax.fori_loop(0, 8, slots, 0, unroll=4)


def unpack(field, parts, out):
    held = [] if out is None else [out]
    return pl.pallas_call(
        unpack_kernel,
        out_shape=jax.ShapeDtypeStruct((3, 128, 8, 256), F32),
        grid=(2,),
        in_specs=[
            pl.BlockSpec((64, 512), lambda i: (i, 0))
            if k is None
            else pl.BlockSpec((1, 64, 512), lambda i, k=k: (k, i, 0))
            for _, k in parts
        ]
        + [pl.BlockSpec(memory_space=pl.ANY)] * len(held),
        out_specs=pl.BlockSpec((1, 64, 8, 256), lambda i: (field, i, 0, 0)),
        input_output_aliases={4: 0} if held else {},
        compiler_params=pltpu.CompilerParams(vmem_limit_bytes=12 * 1024 * 1024),
        cost_estimate=pl.CostEstimate(flops=1_000, bytes_accessed=1_000, transcendentals=0),
    )(*(p for p, _ in parts), *held)


def forecast_kernel(got, obs_out, state_out, a_ref, b_ref, seen):
    def fill(t, carry):
        for f in range(3):
            a_ref[f, pl.ds(1 + 8 * t, 8)] = got[t, pl.ds(8 * f, 8)]
        return carry

    lax.fori_loop(0, 32, fill, 0)

    def wrap(ref, f):
        ref[f, 0] = ref[f, ROWS]
        ref[f, ROWS + 1] = ref[f, 1]

    for f in range(3):
        wrap(a_ref, f)

    def step(src, dst):
        def height(t, carry):
            at = t * CHUNK
            eta = src[0, pl.ds(at, CHUNK + 2)]
            column = DEPTH + eta
            plus, minus = pair_shift(column[1:-1] * src[1, pl.ds(at + 1, CHUNK)])
            carried = column * src[2, pl.ds(at, CHUNK + 2)]
            flux = (plus - minus) + (carried[2:] - carried[:-2])
            dst[0, pl.ds(at + 1, CHUNK)] = eta[1:-1] - (0.5 * TSTEP) * flux
            return carry

        lax.fori_loop(0, ROWS // CHUNK, height, 0, unroll=16)
        wrap(dst, 0)

        def momentum(t, carry):
            at = t * CHUNK
            eta = dst[0, pl.ds(at, CHUNK + 2)]
            east = src[1, pl.ds(at, CHUNK + 2)]
            north = src[2, pl.ds(at, CHUNK + 2)]
            eta_p, eta_m = pair_shift(eta[1:-1])
            e_in, n_in = east[1:-1], north[1:-1]

            def advance(field, inner, slope):
                plus, minus = pair_shift(inner)
                grad_x = plus - minus
                grad_y = field[2:] - field[:-2]
                around = plus + minus + field[2:] + field[:-2]
                force = weigh(2.0 * VISCOSITY, around) - weigh(GRAVITY, slope) - (e_in * grad_x + n_in * grad_y)
                return (1.0 - 4.0 * TSTEP * VISCOSITY) * inner + (0.5 * TSTEP) * force

            new_e = advance(east, e_in, eta_p - eta_m) + (TSTEP * CORIOLIS) * n_in
            new_n = advance(north, n_in, eta[2:] - eta[:-2]) - (TSTEP * CORIOLIS) * e_in
            dst[1, pl.ds(at + 1, CHUNK)] = new_e
            dst[2, pl.ds(at + 1, CHUNK)] = new_n
            return carry

        lax.fori_loop(0, ROWS // CHUNK, momentum, 0, unroll=16)
        wrap(dst, 1)
        wrap(dst, 2)

    def two_steps(t, carry):
        step(a_ref, b_ref)
        step(b_ref, a_ref)
        return carry

    lax.fori_loop(0, STEPS // 2, two_steps, 0)

    sub = lax.broadcasted_iota(jnp.int32, (8, 128), 0)
    lane = lax.broadcasted_iota(jnp.int32, (8, 128), 1)
    low = sub < 4
    first = lane < 64

    def tile_row(r, carry):
        rows = [a_ref[k // 8, 1 + 8 * r + k % 8] for k in range(24)]
        for p in range(2):
            cells = jnp.where(low, got[r, 24, pl.ds(p, 1)], got[r, 24, pl.ds(p + 2, 1)]).astype(jnp.int32)
            at = (cells & 63) + 64 * p
            which = cells >> 6
            value = jnp.zeros((8, 128), F32)
            for k in range(24):
                picked = jnp.take_along_axis(rows[k], at, axis=1, mode="promise_in_bounds")
                value = jnp.where(which == k, picked, value)
            seen[r, p, 0] = value
            seen[r, p, 1] = pltpu.roll(value, 4, 0)
        for j in range(6):
            v = rows[4 * j : 4 * j + 4]
            for p in range(2):
                halves = []
                for g in range(2):
                    x, y = v[2 * g], v[2 * g + 1]
                    if p == 0:
                        halves.append(jnp.where(first, x, pltpu.roll(y, 64, 1)))
                    else:
                        halves.append(jnp.where(first, pltpu.roll(x, 64, 1), y))
                x, y = halves
                state_out[p * 32 + r, :, pl.ds(128 * j, 128)] = jnp.where(low, x, pltpu.roll(y, 4, 0))
                state_out[(2 + p) * 32 + r, :, pl.ds(128 * j, 128)] = jnp.where(low, pltpu.roll(x, 4, 0), y)
        return carry

    lax.fori_loop(0, 32, tile_row, 0, unroll=4)

    def near_row(r, carry):
        for c in range(4):
            outer = (c + 3) % 4 if c % 2 == 0 else (c + 1) % 4
            for j in range(3):
                half = []
                for g in range(2):
                    u = 2 * j + g
                    row = lax.rem(r + u % 3 + 31, 32)
                    tile = c if u < 3 else outer
                    half.append(seen[row, tile % 2, int(tile // 2 != g)])
                obs_out[c * 32 + r, :, pl.ds(128 * j, 128)] = jnp.where(low, half[0], half[1])
        return carry

    lax.fori_loop(0, 32, near_row, 0)


def by_member(msg, j, g):
    block = msg[:, :, pl.ds(128 * j, 128)].reshape(64, 2, 8, 128)
    x, y = block[:, 0], block[:, 1]
    low = lax.broadcasted_iota(jnp.int32, x.shape, 1) < 4
    if g == 0:
        out = jnp.where(low, x, pltpu.roll(y, 4, 1))
    else:
        out = jnp.where(low, pltpu.roll(x, 4, 1), y)
    return out.reshape(COUNT, 128)


def halves(x):
    high = x.astype(BF16)
    return high, (x - high.astype(F32)).astype(BF16)


def times(a, b):
    return lax.dot_general(a, b, (((1,), (0,)), ((), ())), preferred_element_type=F32)


def times_t(a, b):
    return lax.dot_general(a, b, (((1,), (1,)), ((), ())), preferred_element_type=F32)


def full(a, b):
    return jnp.dot(a, b, precision=lax.Precision.HIGHEST, preferred_element_type=F32)


def full_t(a, b):
    dims = (((1,), (1,)), ((), ()))
    return lax.dot_general(a, b, dims, precision=lax.Precision.HIGHEST, preferred_element_type=F32)


def product(a, b, op):
    (ah, al), (bh, bl) = a, b
    return op(ah, bh) + (op(ah, bl) + op(al, bh))


def solve_kernel(obs, obs_core, c_mid, c_side, o_mid, o_side, p_mid, p_side, mix, *scratch):
    spread, misfit, gh, gl, xh, xl, near, sem = scratch
    copies = []
    for i, (mid, side) in enumerate(((c_mid, c_side), (o_mid, o_side), (p_mid, p_side))):
        for row, source in enumerate((side.at[0], mid, side.at[1])):
            copies.append(pltpu.make_async_copy(source, near.at[i, row], sem.at[3 * i + row]))
    for copy in copies:
        copy.start()
    for copy in copies:
        copy.wait()
    for t in range(NEAR):
        source, u = (obs, t) if t < 6 else (obs_core, t - 6)
        seen = by_member(source, u // 2, u % 2)
        place = t // 3, t % 3
        noise = near[place + (slice(0, COUNT),)]
        values = near[place + (slice(COUNT, COUNT + 1),)]
        scale = 1.0 / jnp.sqrt(near[place + (slice(COUNT + 1, COUNT + 2),)])
        mean = jnp.sum(seen, axis=0, keepdims=True) * (1.0 / COUNT)
        at = pl.ds(128 * t, 128)
        spread[:, at] = (seen - mean) * scale
        misfit[:, at] = (values - seen) * scale + noise

    rows = lax.broadcasted_iota(jnp.int32, (COUNT, COUNT), 0)
    cols = lax.broadcasted_iota(jnp.int32, (COUNT, COUNT), 1)
    eye = (rows == cols).astype(F32)
    gram = full_t(spread[...], spread[...]) * (1.0 / (COUNT - 1)) + eye
    gh[...], gl[...] = halves(gram)
    bound = jnp.max(jnp.sum(jnp.abs(gram), axis=1))
    alpha = 2.0 / (1.0 + bound)
    xh[...], xl[...] = halves(alpha * (2.0 * eye - alpha * gram))
    start = 4.0 * bound / ((1.0 + bound) * (1.0 + bound))

    def newton(scale):
        x = (xh[...], xl[...])
        t = product((gh[...], gl[...]), x, times)
        y = product(x, halves(t), times)
        full = x[0].astype(F32) + x[1].astype(F32)
        return scale * (2.0 * full - scale * y)

    def body(low):
        xh[...], xl[...] = halves(newton(2.0 / (1.0 + low)))
        return 4.0 * low / ((1.0 + low) * (1.0 + low))

    lax.while_loop(lambda low: low < 0.9999, body, start)
    inverse = newton(1.0)
    for _ in range(2):
        rest = eye - full(gram, inverse)
        inverse = inverse + product(halves(inverse), halves(rest), times)
    cross = full_t(misfit[...], spread[...]) * (1.0 / (COUNT - 1))
    rows_of = full(cross, inverse) + eye
    me = lax.axis_index("members")
    for k in range(4):
        block = rows_of[128 * k : 128 * (k + 1)]
        at = pl.ds(pl.multiple_of(128 * (me ^ k), 128), 128)
        mix[0, at], mix[1, at] = halves(block)


def apply_kernel(core_first, state, mix, keep, one, two):
    weights = (mix[0], mix[1])
    x = jnp.concatenate([by_member(state, 0, 0), by_member(state, 0, 1)], axis=1)
    mean = jnp.sum(x, axis=0, keepdims=True) * (1.0 / COUNT)
    done = mean + product(weights, halves(x - mean), times)
    lone, first = (256, 128) if core_first else (128, 256)
    keep[...] = done[0:128]
    one[...] = done[lone : lone + 128]
    two[0] = done[first : first + 128]
    two[1] = done[384:512]


def apply(field, state, mix, core_first=False):
    block = jax.ShapeDtypeStruct((128, 512), F32)
    whole = pl.BlockSpec((2, COUNT, COUNT), lambda i: (0, 0, 0))
    flat = pl.BlockSpec((128, 256), lambda i: (0, i))
    return pl.pallas_call(
        functools.partial(apply_kernel, core_first),
        out_shape=[block, block, jax.ShapeDtypeStruct((2, 128, 512), F32)],
        grid=(2,),
        in_specs=[pl.BlockSpec((128, 8, 128), lambda i: (0, 0, 2 * field + i)), whole],
        out_specs=[flat, flat, pl.BlockSpec((2, 128, 256), lambda i: (0, 0, i))],
        compiler_params=pltpu.CompilerParams(vmem_limit_bytes=60 * 1024 * 1024),
        cost_estimate=pl.CostEstimate(flops=10_000_000_000, bytes_accessed=4_000_000, transcendentals=0),
    )(state, mix)


def vmem(n):
    return [pl.BlockSpec(memory_space=pltpu.VMEM)] * n


def call(kernel, shapes, args, scratch=(), flops=0, mib=24, far=0):
    return pl.pallas_call(
        kernel,
        out_shape=shapes,
        in_specs=vmem(len(args) - far) + [pl.BlockSpec(memory_space=pl.ANY)] * far,
        out_specs=vmem(len(shapes)) if isinstance(shapes, (list, tuple)) else vmem(1)[0],
        scratch_shapes=list(scratch),
        compiler_params=pltpu.CompilerParams(vmem_limit_bytes=mib * 1024 * 1024),
        cost_estimate=pl.CostEstimate(flops=flops, bytes_accessed=6_000_000, transcendentals=0),
    )(*args)


def around(x, axis):
    n = lax.axis_size(axis)
    ahead = [(i, (i + 1) % n) for i in range(n)]
    back = [((i + 1) % n, i) for i in range(n)]
    return lax.ppermute(x, axis, ahead), lax.ppermute(x, axis, back)


def local(ensemble, obs_cells, obs_values, obs_var, obs_noise, assign):
    everywhere = ("members", "space")
    me = lax.axis_index("members")
    own = obs_cells.reshape(1, 128).astype(F32)
    other = lax.ppermute(own, "members", [(0, 1), (1, 0), (2, 3), (3, 2)])
    pair = jnp.where(me % 2 == 0, jnp.concatenate([own, other]), jnp.concatenate([other, own]))
    other = lax.ppermute(pair, "members", [(0, 2), (2, 0), (1, 3), (3, 1)])
    cells = jnp.where(me < 2, jnp.concatenate([pair, other] * 2), jnp.concatenate([other, pair] * 2))
    send = pl.pallas_call(
        pack_kernel,
        out_shape=jax.ShapeDtypeStruct((32, 25, 8, 128), F32),
        in_specs=[pl.BlockSpec(memory_space=pl.ANY)],
        out_specs=pl.BlockSpec(memory_space=pl.ANY),
        scratch_shapes=[
            pltpu.VMEM((3, 128, 8, 256), F32),
            pltpu.VMEM((32, 25, 8, 128), F32),
            pltpu.SemaphoreType.DMA((PACK,)),
            pltpu.SemaphoreType.DMA((PACK,)),
        ],
        compiler_params=pltpu.CompilerParams(vmem_limit_bytes=60 * 1024 * 1024),
    )(ensemble)
    send = send.at[:, 24].set(jnp.broadcast_to(cells, (32, 8, 128)))
    got = lax.all_to_all(send, "space", 0, 0, tiled=True)

    noise = jnp.take(obs_noise.reshape(COUNT, 128), assign, axis=0)
    extra = jnp.concatenate([noise, obs_values.reshape(1, 128), obs_var.reshape(1, 128), jnp.zeros((6, 128), F32)])
    core = [(0, 1), (1, 0), (2, 3), (3, 2)]
    chip = [(0, 2), (2, 0), (1, 3), (3, 1)]
    outer = [(0, 3), (3, 0), (1, 2), (2, 1)]
    sides = jnp.stack(around(extra, "space"))
    extra_out = lax.ppermute(extra, "members", outer)
    got, sides, extra_out = lax.optimization_barrier((got, sides, extra_out))
    sides_out = lax.ppermute(sides, "members", outer)

    obs_send, state_send = call(
        forecast_kernel,
        [jax.ShapeDtypeStruct((128, 8, 384), F32), jax.ShapeDtypeStruct((128, 8, 768), F32)],
        (got,),
        [pltpu.VMEM((3, ROWS + 2, 8, 128), F32)] * 2 + [pltpu.VMEM((32, 2, 2, 8, 128), F32)],
        flops=60_000_000,
    )
    obs_send, sides_out = lax.optimization_barrier((obs_send, sides_out))
    obs = lax.all_to_all(obs_send, everywhere, 0, 0, tiled=True)
    state_send, obs = lax.optimization_barrier((state_send, obs))
    state = lax.all_to_all(state_send, everywhere, 0, 0, tiled=True)
    obs, extra, sides = lax.optimization_barrier((obs, extra, sides))
    obs_core = lax.ppermute(obs[:, :, 0:256], "members", core)
    extra_core = lax.ppermute(extra, "members", core)
    sides_core = lax.ppermute(sides, "members", core)
    mix = call(
        solve_kernel,
        jax.ShapeDtypeStruct((2, COUNT, COUNT), BF16),
        (obs, obs_core, extra, sides, extra_out, sides_out, extra_core, sides_core),
        [pltpu.VMEM((COUNT, 128 * NEAR), F32)] * 2
        + [pltpu.VMEM((COUNT, COUNT), BF16)] * 4
        + [pltpu.VMEM((3, 3, 520, 128), F32), pltpu.SemaphoreType.DMA((9,))],
        flops=20_000_000_000,
        far=6,
        mib=32,
    )
    sets = []
    for field in range(2):
        keep, near, far = apply(field, state, mix)
        sets.append((keep, near, lax.ppermute(far, "members", chip)))
    keep, far, pair = apply(2, state, mix, core_first=True)
    pair = lax.ppermute(pair, "members", core)
    far = jnp.stack([far, pair[1]])
    last = lax.ppermute(far, "members", chip)
    far_0, _ = lax.optimization_barrier((sets[0][2], far))
    near_0, near_1, far_0 = lax.optimization_barrier((sets[0][1], sets[1][1], far_0))
    near_0 = lax.ppermute(near_0, "members", core)
    near_1 = lax.ppermute(near_1, "members", core)
    cross = lax.ppermute(far_0[1], "members", core)
    out = unpack(0, ((sets[0][0], None), (near_0, None), (far_0, 0), (cross, None)), None)
    far_1, out = lax.optimization_barrier((sets[1][2], out))
    cross = lax.ppermute(far_1[1], "members", core)
    out = unpack(1, ((sets[1][0], None), (near_1, None), (far_1, 0), (cross, None)), out)
    last, out = lax.optimization_barrier((last, out))
    return unpack(2, ((keep, None), (pair, 0), (last, 0), (last, 1)), out)


def solution(mesh):
    placed = (
        P(None, "members", "space", None),
        P("space", "members", None),
        P("space", "members", None),
        P("space", "members", None),
        P(None, "space", "members", None),
        P(),
    )
    return jax.shard_map(
        local,
        mesh=mesh,
        in_specs=placed,
        out_specs=P(None, "members", "space", None),
        check_vma=False,
    )
```
